1024 devices in a mesh: dp: 128 (over y, z), tensor: 8 (over x, core).
Axes of the slice: x: 4, y: 4, z: 32, core: 2. Of those that a mesh axis runs over, the one named last changes fastest.
Arguments:
- gradient: bfloat16 [56, 512, 512], P(None, 'dp', 'tensor'), may hold values from -100 to 100
- second_moment: float32 [56, 512, 512], P(None, 'dp', 'tensor'), may hold values from 0 to 64
- factors: bfloat16 [56, 2, 512, 512], P(None, None, 'dp', 'tensor'), may hold values from -2 to 2, as said below
- old_owner: int32 [56], replicated, may hold values from 0 to 127, as said below
- new_owner: int32 [56], replicated, may hold values from 0 to 127, as said below
- offsets: int32 [56], replicated, may hold values from 0 to 55, each once
Outputs:
- direction: bfloat16 [56, 512, 512], P(None, 'dp', 'tensor')
- moment_new: float32 [56, 512, 512], P(None, 'dp', 'tensor')
- owner_grafts: float32 [128, 2], P('dp')
The draws below stay inside these ranges and needn't reach their ends.
Inputs may be any that keep to these rules, and one draw needn't show every extreme that they name: `old_owner`: each device of dp owned at most 2 blocks, and one owned exactly 2. `new_owner`: each device of dp owns at most 2 blocks, and one owns exactly 2. Every block factors[s, i] is symmetric.
All inputs are finite; a program needn't handle non-finite values.
Results may differ from the reference program's by a relative error of at most 0.0057.
Values may be sent and summed in bfloat16 or wider, within the bound.
No kernel may reach another device: no remote copies, remote signals or barrier semaphores. Data moves between devices by JAX's collectives and lax.ppermute only.
A program may use at most 64 MiB of HBM per device.

```python
import math
import jax
import jax.numpy as jnp
from jax import lax

BLOCK = 512
BLOCKS = 56
CAPACITY = 2
N_DP = 128


def owner_list(key):
    most_held = max(2, 2 * BLOCKS // N_DP)
    key_order, key_spare, key_shuffle = jax.random.split(key, 3)
    owner_order = jax.random.permutation(key_order, N_DP)
    spare_slots = jax.random.permutation(key_spare, (N_DP - 1) * most_held)[:BLOCKS - most_held]
    others = owner_order[1 + spare_slots // most_held].astype(jnp.int32)
    owners = jnp.concatenate([jnp.full((most_held,), owner_order[0], jnp.int32), others])
    shuffle = jax.random.permutation(key_shuffle, BLOCKS)
    return owners[shuffle].astype(jnp.int32)


def draw_old_owner(key, part):
    key = jax.random.fold_in(key, 11)
    return owner_list(key)


def draw_new_owner(key, part):
    key = jax.random.fold_in(key, 12)
    return owner_list(key)


def draw_gradient(key, part):
    key = jax.random.fold_in(key, 21)
    key_noise, key_rows, key_cols = jax.random.split(key, 3)
    full_shape = (BLOCKS, BLOCK, BLOCK)
    spread = math.log(10.0) / 2.0
    values = jax.random.truncated_normal(key_noise, -5.0, 5.0, full_shape, jnp.float32)
    row_scale = jnp.exp(jax.random.uniform(key_rows, (BLOCKS, BLOCK, 1), jnp.float32, -spread, spread))
    col_scale = jnp.exp(jax.random.uniform(key_cols, (BLOCKS, 1, BLOCK), jnp.float32, -spread, spread))
    return (values * row_scale * col_scale).astype(jnp.bfloat16)


def draw_second_moment(key, part):
    key = jax.random.fold_in(key, 31)
    key_noise, key_block, key_rows, key_cols = jax.random.split(key, 4)
    full_shape = (BLOCKS, BLOCK, BLOCK)
    lower_scale, upper_scale = (0.1, 1.0)
    noise_part = jnp.exp(jax.random.uniform(key_noise, full_shape, jnp.float32, math.log(0.5), math.log(2.0)))
    block_scale = jnp.exp(jax.random.uniform(key_block, (BLOCKS, 1, 1), jnp.float32, math.log(lower_scale), math.log(upper_scale)))
    row_scale = jnp.exp(jax.random.uniform(key_rows, (BLOCKS, BLOCK, 1), jnp.float32, math.log(0.3), math.log(3.3)))
    col_scale = jnp.exp(jax.random.uniform(key_cols, (BLOCKS, 1, BLOCK), jnp.float32, math.log(0.3), math.log(3.3)))
    return (block_scale * row_scale * col_scale * noise_part).astype(jnp.float32)


def draw_factors(key, part):
    key = jax.random.fold_in(key, 41)
    key_off, key_diag = jax.random.split(key, 2)
    full_shape = (BLOCKS, 2, BLOCK, BLOCK)
    raw_entries = jax.random.truncated_normal(key_off, -5.0, 5.0, full_shape, jnp.float32)
    diag_low, diag_high = (0.8, 1.6)
    symmetric = (raw_entries + jnp.swapaxes(raw_entries, 2, 3)) * (0.35 / math.sqrt(2.0 * BLOCK))
    diagonal = jax.random.uniform(key_diag, (BLOCKS, 2, BLOCK, 1), jnp.float32, diag_low, diag_high)
    positions = jnp.arange(BLOCK, dtype=jnp.int32)
    on_diagonal = positions[:, None] == positions[None, :]
    return jnp.where(on_diagonal, diagonal, symmetric).astype(jnp.bfloat16)


def setup_inputs(seed: int = 0) -> dict:
    key_of = jax.random.split(jax.random.key(seed), 7)
    return {
        "gradient": draw_gradient(jax.random.fold_in(key_of[6], 71), 0),
        "second_moment": draw_second_moment(jax.random.fold_in(key_of[6], 71), 0),
        "factors": draw_factors(jax.random.fold_in(key_of[6], 71), 0),
        "old_owner": draw_old_owner(jax.random.fold_in(key_of[6], 71), 0),
        "new_owner": draw_new_owner(jax.random.fold_in(key_of[6], 71), 0),
        "offsets": jax.random.permutation(key_of[5], BLOCKS).astype(jnp.int32),
    }


BETA_TWO = 0.99
ADAM_EPS = 1e-08
NORM_EPS = 1e-06

def checkpoint_slots(old_owner):
    positions = jnp.arange(old_owner.shape[0], dtype=jnp.int32)
    before = old_owner[None, :] < old_owner[:, None]
    tied_before = (old_owner[None, :] == old_owner[:, None]) & (positions[None, :] < positions[:, None])
    return lax.optimization_barrier(jnp.sum((before | tied_before).astype(jnp.int32), axis=1)).astype(jnp.int32)

def owner_ranks(new_owner):
    positions = jnp.arange(new_owner.shape[0], dtype=jnp.int32)
    tied_before = (new_owner[None, :] == new_owner[:, None]) & (positions[None, :] < positions[:, None])
    return lax.optimization_barrier(jnp.sum(tied_before.astype(jnp.int32), axis=1)).astype(jnp.int32)

def reference(gradient, second_moment, factors, old_owner, new_owner, offsets):
    wide_grad = gradient.astype(jnp.float32)
    moment_new = BETA_TWO * second_moment + (1.0 - BETA_TWO) * wide_grad * wide_grad
    adam_step = wide_grad / (jnp.sqrt(moment_new) + ADAM_EPS)
    adam_sq = lax.optimization_barrier(jnp.sum(adam_step * adam_step, axis=(1, 2)))
    ckpt_slots = checkpoint_slots(old_owner)
    left_factor = factors[ckpt_slots, 0]
    right_factor = factors[ckpt_slots, 1]
    block_grad = gradient[offsets]
    product = jnp.einsum('bik,bjk->bij', right_factor.astype(jnp.float32), block_grad.astype(jnp.float32)).astype(jnp.bfloat16)
    transposed = jnp.einsum('bij,bjr->bir', product.astype(jnp.float32), left_factor.astype(jnp.float32)).astype(jnp.bfloat16)
    shampoo = jnp.swapaxes(transposed, 1, 2)
    wide_shampoo = shampoo.astype(jnp.float32)
    shampoo_sq = lax.optimization_barrier(jnp.sum(wide_shampoo * wide_shampoo, axis=(1, 2)))
    graft_scale = jnp.sqrt(adam_sq[offsets] / (shampoo_sq + NORM_EPS))
    block_dir = (graft_scale[:, None, None] * wide_shampoo).astype(jnp.bfloat16)
    direction = jnp.zeros(gradient.shape, jnp.bfloat16).at[offsets].set(block_dir)
    owner_grafts = jnp.zeros((N_DP, CAPACITY), jnp.float32).at[new_owner, owner_ranks(new_owner)].set(graft_scale)
    return (direction, moment_new, owner_grafts)
```

```python
import jax
import jax.numpy as jnp
from jax import lax
from jax.experimental import pallas as pl
from jax.experimental.pallas import tpu as pltpu
from jax.sharding import Mesh
from jax.sharding import PartitionSpec as P

BETA_TWO = 0.99
ADAM_EPS = 1e-08
NORM_EPS = 1e-06
F32 = jnp.float32
BF16 = jnp.bfloat16
NB = 56
NZ = 32
VMEM = pl.BlockSpec(memory_space=pltpu.VMEM)
ANY = pl.BlockSpec(memory_space=pl.ANY)
SMEM = pl.BlockSpec(memory_space=pltpu.SMEM)


def iota(shape, dim):
    return lax.broadcasted_iota(jnp.int32, shape, dim)


def total(mask, values, axis):
    picked = jnp.where(mask, values.astype(F32), 0.0)
    return jnp.sum(picked, axis=axis, keepdims=True).astype(jnp.int32)


def one_hot(mask):
    return jnp.where(mask, 1.0, 0.0).astype(BF16)


def pick(mask, rows):
    return jnp.dot(one_hot(mask), rows, preferred_element_type=F32)


def to_column(row):
    sub, lane = iota((NB, NB), 0), iota((NB, NB), 1)
    return total(sub == lane, jnp.broadcast_to(row, (NB, NB)), 1)


def tied_before(row, column):
    sub, lane = iota((NB, NB), 0), iota((NB, NB), 1)
    return total((column == row) & (sub < lane), jnp.ones((NB, NB), jnp.int32), 0)


def slots_row(row, column):
    sub, lane = iota((NB, NB), 0), iota((NB, NB), 1)
    before = (column < row) | ((column == row) & (sub < lane))
    return total(before, jnp.ones((NB, NB), jnp.int32), 0)


def split_three(x):
    high = x.astype(BF16).astype(F32)
    rest = x - high
    mid = rest.astype(BF16).astype(F32)
    return high, mid, (rest - mid).astype(BF16).astype(F32)


def pack_kernel(
    coord_ref, grad_hbm, moment_hbm, factor_hbm, old_hbm, own_hbm, off_hbm,
    new_ref, send_ref, table_ref,
    grad_ref, moment_ref, factor_ref, old_ref, own_ref, off_ref, sems,
):
    pairs = (
        (old_hbm, old_ref),
        (off_hbm, off_ref),
        (own_hbm, own_ref),
        (grad_hbm, grad_ref),
        (moment_hbm, moment_ref),
        (factor_hbm, factor_ref),
    )
    copies = [pltpu.make_async_copy(src, dst, sems.at[i]) for i, (src, dst) in enumerate(pairs)]
    for copy in copies:
        copy.start()
    for copy in copies[:3]:
        copy.wait()
    old, own = old_ref[...], own_ref[...]
    slot = slots_row(old, to_column(old))
    slot_col, off_col = to_column(slot), to_column(off_ref[...])
    lane56 = iota((NB, NB), 1)
    position = total(slot_col == lane56, jnp.broadcast_to(off_col, (NB, NB)), 0)
    at = total(off_col == lane56, jnp.broadcast_to(slot_col, (NB, NB)), 0)
    rank = tied_before(own, to_column(own))
    held = own == coord_ref[0]
    first_row = ((slot & 1) * NZ + (slot >> 1)) * 4
    table_ref[0:1, 0:NB] = at
    for k in range(2):
        table_ref[k + 1 : k + 2, 0:NB] = jnp.where(held & (rank == k), first_row, -1)
    rows = 8 * NB
    row = iota((rows, NB), 0)
    spread = total(
        iota((rows, NB), 1) == (row >> 3), jnp.broadcast_to(position, (rows, NB)), 1
    )
    r = iota((rows, 1), 0) & 7
    source = spread * 4 + (r & 3) + 4 * NB * (r >> 2)
    for copy in copies[3:]:
        copy.wait()
    grad = grad_ref[...]
    wide = grad.astype(F32)
    moment = BETA_TWO * moment_ref[...] + (1.0 - BETA_TWO) * wide * wide
    new_ref[...] = moment
    step = wide / (jnp.sqrt(moment) + ADAM_EPS)
    high, mid, low = split_three(jnp.sum(step * step, axis=1, keepdims=True))
    lane = iota((4 * NB, 64), 1)
    sums = jnp.where(lane == 0, high, jnp.where(lane == 1, mid, jnp.where(lane == 2, low, 0.0)))
    stacked = jnp.concatenate([grad, sums.astype(BF16)], axis=0)
    mine = pick(iota((rows, rows), 1) == source, stacked).astype(BF16)
    send_ref[0:rows, :] = jnp.concatenate([factor_ref[...], mine], axis=1)
    send_ref[rows:, :] = jnp.zeros((16 * NZ - rows, 128), BF16)


def three_lanes(x, shape, first):
    lane = iota(shape, 1) - first
    high, mid, low = split_three(x)
    return jnp.where(lane == 0, high, jnp.where(lane == 1, mid, jnp.where(lane == 2, low, 0.0)))


def whole_sum(x):
    return jnp.sum(jnp.sum(x, axis=0, keepdims=True), axis=1, keepdims=True)


def spread_kernel(in_ref, out_ref):
    n = 16 * NZ
    got = in_ref[...]
    o, k = iota((256, n), 0), iota((256, n), 1)
    pairs = pick(k == ((o >> 2) & 31) * 16 + (o >> 7) * 8 + (o & 3), got).astype(BF16)
    o, k = iota((128, n), 0), iota((128, n), 1)
    near = ((o >> 2) & 15) * 16 + (o >> 6) * 8 + 4 + (o & 3)
    right = jnp.concatenate(
        [pick(k == near, got)[:, :64], pick(k == near + 256, got)[:, :64]], axis=1
    ).astype(BF16)
    r, lane = iota((n, 128), 0) & 15, iota((n, 128), 1)
    sums = jnp.where(lane >= 64, got.astype(F32), 0.0)
    for e in range(2):
        adam = whole_sum(jnp.where((r >= 8 * e + 4) & (r < 8 * e + 8), sums, 0.0))
        adam = jnp.where(iota((16, 128), 0) == 0, three_lanes(adam, (16, 128), 0), 0.0).astype(BF16)
        for dest in range(16):
            if (dest // 4) % 2 == e:
                out_ref[dest, 0:128] = pairs[128 * e : 128 * e + 128]
                out_ref[dest, 128:192] = right[64 * e : 64 * e + 64]
                out_ref[dest, 192:208] = adam


def block_kernel(coord_ref, own_ref, other_ref, out_ref, left, right, grad, parts):
    yh, x, c = coord_ref[1], coord_ref[2], coord_ref[3]
    sums = jnp.zeros((16, 128), F32)
    for yy in range(4):
        for xx in range(4):
            i = yy * 4 + xx
            rr, cc = slice(128 * yy, 128 * yy + 128), slice(128 * xx, 128 * xx + 128)
            a0, a1 = own_ref[i, 0:128, :], other_ref[i, 0:128, :]
            low = jnp.where(c == 0, a0[:, :64], a1[:, :64])
            high = jnp.where(c == 0, a1[:, :64], a0[:, :64])
            left[rr, cc] = jnp.concatenate([low, high], axis=1)
            grad[rr, cc] = jnp.concatenate([a0[:, 64:], a1[:, 64:]], axis=1)
            b0, b1 = own_ref[i, 128:192, :], other_ref[i, 128:192, :]
            mid = 128 * yy + 64
            right[128 * yy : mid, cc] = jnp.concatenate([b0[:, :64], b1[:, :64]], axis=1)
            right[mid : mid + 64, cc] = jnp.concatenate([b0[:, 64:], b1[:, 64:]], axis=1)
            sums = sums + own_ref[i, 192:208, :].astype(F32) + other_ref[i, 192:208, :].astype(F32)
    lanes = (((1,), (1,)), ((), ()))
    product = lax.dot_general(right[...], grad[...], lanes, preferred_element_type=F32).astype(BF16)
    shampoo = lax.dot_general(left[...], product, lanes, preferred_element_type=F32).astype(BF16)
    wide = shampoo.astype(F32)
    scale = jnp.sqrt(whole_sum(sums) / (whole_sum(wide * wide) + NORM_EPS))
    direction = (scale * wide).astype(BF16)
    for hh in range(2):
        for xx in range(4):
            parts[4 * hh + xx] = direction[256 * hh : 256 * hh + 256, 128 * xx : 128 * xx + 128]
    mine = parts[4 * yh + x]
    mine = jnp.where(c == 0, mine[:, :64], mine[:, 64:])
    out_ref[...] = jnp.concatenate([mine, three_lanes(scale, (256, 64), 0).astype(BF16)], axis=1)


def unpack_kernel(table_ref, in_ref, dir_ref, graft_ref):
    got = in_ref[...]
    rows = 4 * NB
    row = iota((rows, NB), 0)
    at = jnp.broadcast_to(table_ref[0:1, 0:NB], (rows, NB))
    s = total(iota((rows, NB), 1) == (row >> 2), at, 1)
    source = ((s & 1) * NZ + (s >> 1)) * 4 + (iota((rows, 1), 0) & 3)
    dir_ref[...] = pick(iota((rows, 256), 1) == source, got[:, :64]).astype(BF16)
    scales = jnp.sum(got[:, 64:].astype(F32), axis=1, keepdims=True)
    grafts = []
    for k in range(2):
        hit = iota((256, NB), 0) == table_ref[k + 1 : k + 2, 0:NB]
        grafts.append(whole_sum(jnp.where(hit, jnp.broadcast_to(scales, (256, NB)), 0.0)))
    graft_ref[...] = jnp.where(iota((1, 2), 1) == 0, grafts[0], grafts[1])


def per_device(gradient, second_moment, factors, old_owner, new_owner, offsets):
    rank = lax.axis_index(("yh", "yl", "z"))
    coords = jnp.stack([rank, lax.axis_index("yh"), lax.axis_index("x"), lax.axis_index("c")])
    coords = coords.astype(jnp.int32)
    old, own, off = (a.reshape(1, NB) for a in (old_owner, new_owner, offsets))
    params = pltpu.CompilerParams(vmem_limit_bytes=40 * 1024 * 1024)
    with jax.named_scope("pack"):
        moment_new, send, table = pl.pallas_call(
            pack_kernel,
            out_shape=(
                jax.ShapeDtypeStruct((4 * NB, 64), F32),
                jax.ShapeDtypeStruct((16 * NZ, 128), BF16),
                jax.ShapeDtypeStruct((8, 128), jnp.int32),
            ),
            in_specs=[SMEM] + [ANY] * 6,
            out_specs=(VMEM, VMEM, VMEM),
            scratch_shapes=[
                pltpu.VMEM((4 * NB, 64), BF16),
                pltpu.VMEM((4 * NB, 64), F32),
                pltpu.VMEM((8 * NB, 64), BF16),
                pltpu.VMEM((1, NB), jnp.int32),
                pltpu.VMEM((1, NB), jnp.int32),
                pltpu.VMEM((1, NB), jnp.int32),
                pltpu.SemaphoreType.DMA((6,)),
            ],
            compiler_params=pltpu.CompilerParams(vmem_limit_bytes=60 * 1024 * 1024),
        )(
            coords,
            gradient.reshape(4 * NB, 64),
            second_moment.reshape(4 * NB, 64),
            factors.reshape(8 * NB, 64),
            old,
            own,
            off,
        )
    with jax.named_scope("to_planes"):
        got = lax.all_to_all(send.reshape(NZ, 16, 128), "z", 0, 0, tiled=True)
    with jax.named_scope("spread"):
        send = pl.pallas_call(
            spread_kernel,
            out_shape=jax.ShapeDtypeStruct((16, 208, 128), BF16),
            in_specs=[VMEM],
            out_specs=VMEM,
            compiler_params=params,
        )(got.reshape(16 * NZ, 128))
    with jax.named_scope("in_plane"):
        got = lax.all_to_all(send, ("yh", "yl", "x"), 0, 0, tiled=True)
    with jax.named_scope("cores"):
        other = lax.ppermute(got, "c", [(0, 1), (1, 0)])
    with jax.named_scope("block"):
        send = pl.pallas_call(
            block_kernel,
            out_shape=jax.ShapeDtypeStruct((256, 128), BF16),
            in_specs=[SMEM, VMEM, VMEM],
            out_specs=VMEM,
            scratch_shapes=[pltpu.VMEM((512, 512), BF16)] * 3 + [pltpu.VMEM((8, 256, 128), BF16)],
            compiler_params=params,
        )(coords, got, other)
    with jax.named_scope("back"):
        got = lax.all_to_all(send.reshape(64, 4, 128), ("yl", "z"), 0, 0, tiled=True)
    with jax.named_scope("unpack"):
        direction, grafts = pl.pallas_call(
            unpack_kernel,
            out_shape=(
                jax.ShapeDtypeStruct((4 * NB, 64), BF16),
                jax.ShapeDtypeStruct((1, 2), F32),
            ),
            in_specs=[VMEM, VMEM],
            out_specs=(VMEM, VMEM),
            compiler_params=params,
        )(table, got.reshape(256, 128))
    return (direction.reshape(NB, 4, 64), moment_new.reshape(NB, 4, 64), grafts)


def solution(mesh):
    split = Mesh(mesh.devices.reshape(2, 2, NZ, 4, 2), ("yh", "yl", "z", "x", "c"))
    dp, tensor = ("yh", "yl", "z"), ("x", "c")
    flat = P(None, dp, tensor)
    return jax.shard_map(
        per_device,
        mesh=split,
        in_specs=(flat, flat, P(None, None, dp, tensor), P(), P(), P()),
        out_specs=(flat, flat, P(dp, None)),
        check_vma=False,
    )
```

```python
import jax
import jax.numpy as jnp
from jax import lax
from jax.experimental import pallas as pl
from jax.experimental.pallas import tpu as pltpu
from jax.sharding import Mesh
from jax.sharding import PartitionSpec as P

BETA_TWO = 0.99
ADAM_EPS = 1e-08
NORM_EPS = 1e-06
F32 = jnp.float32
BF16 = jnp.bfloat16
NB = 56
NZ = 32
SENDROWS = 10
PLANE_FACTOR = 6554
VMEM = pl.BlockSpec(memory_space=pltpu.VMEM)
ANY = pl.BlockSpec(memory_space=pl.ANY)


def iota(shape, dim):
    return lax.broadcasted_iota(jnp.int32, shape, dim)


def total(mask, values, axis):
    picked = jnp.where(mask, values.astype(F32), 0.0)
    return jnp.sum(picked, axis=axis, keepdims=True).astype(jnp.int32)


def one_hot(mask):
    return jnp.where(mask, 1.0, 0.0).astype(BF16)


def pick(mask, rows):
    return jnp.dot(one_hot(mask), rows, preferred_element_type=F32)


def to_column(row):
    sub, lane = iota((NB, NB), 0), iota((NB, NB), 1)
    return total(sub == lane, jnp.broadcast_to(row, (NB, NB)), 1)


def to_column_wide(row):
    sub, lane = iota((NB, NB), 0), iota((NB, NB), 1)
    return jnp.sum(jnp.where(sub == lane, jnp.broadcast_to(row, (NB, NB)), 0.0), axis=1, keepdims=True)


def tied_before(row, column):
    sub, lane = iota((NB, NB), 0), iota((NB, NB), 1)
    return total((column == row) & (sub < lane), jnp.ones((NB, NB), jnp.int32), 0)


def slots_row(row, column):
    sub, lane = iota((NB, NB), 0), iota((NB, NB), 1)
    before = (column < row) | ((column == row) & (sub < lane))
    return total(before, jnp.ones((NB, NB), jnp.int32), 0)


def split_three(x):
    high = x.astype(BF16).astype(F32)
    rest = x - high
    mid = rest.astype(BF16).astype(F32)
    return high, mid, (rest - mid).astype(BF16).astype(F32)


def three_lanes(x, lane):
    high, mid, low = split_three(x)
    return jnp.where(lane == 0, high, jnp.where(lane == 1, mid, jnp.where(lane == 2, low, 0.0)))


def whole_sum(x):
    return jnp.sum(jnp.sum(x, axis=0, keepdims=True), axis=1, keepdims=True)


def adam_moment(grad, moment):
    wide = grad.astype(F32)
    return wide, BETA_TWO * moment + (1.0 - BETA_TWO) * wide * wide


def dp_rank():
    return (lax.axis_index("yh") * 2 + lax.axis_index("yl")) * NZ + lax.axis_index("z")


def fetch(pairs, sems):
    copies = [pltpu.make_async_copy(src, dst, sems.at[i]) for i, (src, dst) in enumerate(pairs)]
    for copy in copies:
        copy.start()
    return copies


def pack_kernel(
    grad_hbm, moment_hbm, factor_hbm, old_hbm, off_hbm, send_ref,
    grad_ref, moment_ref, factor_ref, old_ref, off_ref, sems,
):
    copies = fetch(
        (
            (old_hbm, old_ref),
            (off_hbm, off_ref),
            (grad_hbm, grad_ref),
            (moment_hbm, moment_ref),
            (factor_hbm, factor_ref),
        ),
        sems,
    )
    row0 = dp_rank() * 4
    col0 = (lax.axis_index("x") * 2 + lax.axis_index("c")) * 64
    for copy in copies[:2]:
        copy.wait()
    old = old_ref[...]
    slot_col, off_col = to_column(slots_row(old, to_column(old))), to_column(off_ref[...])
    position = total(slot_col == iota((NB, NB), 1), jnp.broadcast_to(off_col, (NB, NB)), 0)
    rows = SENDROWS * NZ
    sent = iota((rows, NB), 0)
    plane = (sent * PLANE_FACTOR) >> 16
    q = sent - SENDROWS * plane
    seat = 2 * plane + ((q >> 2) & 1)
    spread = total(iota((rows, NB), 1) == seat, jnp.broadcast_to(position, (rows, NB)), 1)
    plane, q = plane[:, 0:1], q[:, 0:1]
    r = q & 3
    from_factor = jnp.where(q < 8, (2 * plane + (q >> 2)) * 8 + r, -1)
    from_grad = jnp.where(q < 8, spread * 4 + r, jnp.where(q == 8, 4 * NB + plane, -1)) + 8 * NB
    k = iota((rows, 12 * NB + NZ), 1)
    mask = (k == from_factor) | (k == from_grad)
    for copy in copies[2:]:
        copy.wait()
    grad = grad_ref[...]
    wide, moment = adam_moment(grad, moment_ref[...])
    step = wide / (jnp.sqrt(moment) + ADAM_EPS)
    by_row = jnp.sum(step * step, axis=1, keepdims=True)
    mine = iota((4 * NB, NB), 1) == (iota((4 * NB, NB), 0) >> 2)
    by_block = jnp.sum(jnp.where(mine, by_row, 0.0), axis=0, keepdims=True)
    by_slot = jnp.sum(
        jnp.where(
            iota((NB, NB), 0) == jnp.broadcast_to(position, (NB, NB)), to_column_wide(by_block), 0.0
        ),
        axis=0,
        keepdims=True,
    )
    factor = factor_ref[...].astype(F32)
    r8, lane = iota((8 * NB, 64), 0) & 7, iota((8 * NB, 64), 1)
    row, col = row0 + (r8 & 3), col0 + lane
    right = pltpu.roll(factor, 8 * NB - 4, 0)
    mixed = jnp.where(col > row, factor, right)
    on_diagonal = jnp.sum(jnp.where((col == row) & (r8 < 4), factor, 0.0), axis=1, keepdims=True)
    r8, lane = iota((8 * NB, 128), 0), iota((8 * NB, 128), 1)
    seat_lane = 64 * ((r8 >> 3) & 1) + 8 + (r8 & 3)
    on_diagonal = jnp.where(lane == seat_lane, on_diagonal, 0.0).astype(BF16)
    extra = pick(iota((NZ, 8 * NB), 0) == (iota((NZ, 8 * NB), 1) >> 4), on_diagonal)
    p, s = iota((NZ, NB), 0), iota((NZ, NB), 1)
    for e in range(2):
        adam = jnp.sum(jnp.where(s == 2 * p + e, by_slot, 0.0), axis=1, keepdims=True)
        extra = extra + three_lanes(adam, iota((NZ, 128), 1) - 64 * e)
    none = jnp.zeros((8 * NB, 64), BF16)
    source = jnp.concatenate(
        [
            jnp.concatenate([mixed.astype(BF16), none], axis=1),
            jnp.concatenate([none[: 4 * NB], grad], axis=1),
            extra.astype(BF16),
        ],
        axis=0,
    )
    send_ref[...] = pick(mask, source).astype(BF16)


def moment_kernel(
    after_hbm, grad_hbm, moment_hbm, old_hbm, own_hbm, off_hbm, new_ref, table_ref,
    grad_ref, moment_ref, old_ref, own_ref, off_ref, sems,
):
    del after_hbm
    copies = fetch(
        (
            (old_hbm, old_ref),
            (off_hbm, off_ref),
            (own_hbm, own_ref),
            (grad_hbm, grad_ref),
            (moment_hbm, moment_ref),
        ),
        sems,
    )
    for copy in copies:
        copy.wait()
    new_ref[...] = adam_moment(grad_ref[...], moment_ref[...])[1]
    old, own = old_ref[...], own_ref[...]
    slot = slots_row(old, to_column(old))
    slot_col, off_col = to_column(slot), to_column(off_ref[...])
    at = total(off_col == iota((NB, NB), 1), jnp.broadcast_to(slot_col, (NB, NB)), 0)
    rank = tied_before(own, to_column(own))
    held = own == dp_rank()
    first_row = ((slot & 1) * NZ + (slot >> 1)) * 4
    table_ref[0:1, 0:NB] = at
    for k in range(2):
        table_ref[k + 1 : k + 2, 0:NB] = jnp.where(held & (rank == k), first_row, -1)


def spread_kernel(in_ref, out_ref):
    n = SENDROWS * NZ
    got = in_ref[...]
    o, k = iota((256, n), 0), iota((256, n), 1)
    pairs = pick(k == ((o >> 2) & 31) * SENDROWS + (o >> 7) * 4 + (o & 3), got).astype(BF16)
    o, k = iota((NZ, n), 0), iota((NZ, n), 1)
    extra = pick(k == o * SENDROWS + 8, got).astype(BF16)
    for e in range(2):
        lanes = slice(64 * e, 64 * e + 64)
        rest = jnp.concatenate([extra[:16, lanes], extra[16:, lanes]], axis=1)
        for dest in range(16):
            if (dest // 4) % 2 == e:
                out_ref[dest, 0:128] = pairs[128 * e : 128 * e + 128]
                out_ref[dest, 128:144] = rest


def block_kernel(own_ref, other_ref, table_hbm, out_ref, mixed, grad, parts):
    del table_hbm
    yh, x, c = lax.axis_index("yh"), lax.axis_index("x"), lax.axis_index("c")

    def assemble(low_ref, high_ref):
        for yy in range(4):
            for xx in range(4):
                i = yy * 4 + xx
                rr, cc = slice(128 * yy, 128 * yy + 128), slice(128 * xx, 128 * xx + 128)
                low, high = low_ref[i, 0:128, :], high_ref[i, 0:128, :]
                mixed[rr, cc] = jnp.concatenate([low[:, :64], high[:, :64]], axis=1)
                grad[rr, cc] = jnp.concatenate([low[:, 64:], high[:, 64:]], axis=1)

    @pl.when(c == 0)
    def _():
        assemble(own_ref, other_ref)

    @pl.when(c == 1)
    def _():
        assemble(other_ref, own_ref)

    extras = []
    for yy in range(4):
        parts_of = [ref[4 * yy + xx, 128:144, :].astype(F32) for ref in (own_ref, other_ref) for xx in range(4)]
        extras.append(sum(parts_of[1:], parts_of[0]))
    extra = jnp.concatenate(extras, axis=0)
    lane = iota((64, 128), 1) & 63
    adam_sq = whole_sum(jnp.where(lane < 3, extra, 0.0))
    diagonal = jnp.where(lane < 3, 0.0, extra).astype(BF16)
    i, k = iota((512, 64), 0), iota((512, 64), 1)
    diagonal = pick(k == ((i >> 7) * 16 + ((i >> 2) & 15)), diagonal)
    i, k = iota((512, 128), 0), iota((512, 128), 1)
    seat_lane = ((i >> 6) & 1) * 64 + 8 + (i & 3)
    diagonal = jnp.sum(jnp.where(k == seat_lane, diagonal, 0.0), axis=1, keepdims=True)
    entries = mixed[...].astype(F32)
    turned = entries.T
    row, col = iota((512, 512), 0), iota((512, 512), 1)
    left = jnp.where(col > row, entries, jnp.where(col < row, turned, diagonal)).astype(BF16)
    right = jnp.where(col > row, turned, entries).astype(BF16)
    lanes = (((1,), (1,)), ((), ()))
    product = lax.dot_general(right, grad[...], lanes, preferred_element_type=F32).astype(BF16)
    shampoo = lax.dot_general(left, product, lanes, preferred_element_type=F32).astype(BF16)
    wide = shampoo.astype(F32)
    scale = jnp.sqrt(adam_sq / (whole_sum(wide * wide) + NORM_EPS))
    direction = (scale * wide).astype(BF16)
    for hh in range(2):
        for xx in range(4):
            parts[4 * hh + xx] = direction[256 * hh : 256 * hh + 256, 128 * xx : 128 * xx + 128]
    mine = parts[4 * yh + x]
    mine = jnp.where(c == 0, mine[:, :64], mine[:, 64:])
    out_ref[...] = jnp.concatenate([mine, three_lanes(scale, iota((256, 64), 1)).astype(BF16)], axis=1)


def unpack_kernel(table_ref, in_ref, dir_ref, graft_ref):
    got = in_ref[...]
    rows = 4 * NB
    row = iota((rows, NB), 0)
    at = jnp.broadcast_to(table_ref[0:1, 0:NB], (rows, NB))
    s = total(iota((rows, NB), 1) == (row >> 2), at, 1)
    source = ((s & 1) * NZ + (s >> 1)) * 4 + (iota((rows, 1), 0) & 3)
    dir_ref[...] = pick(iota((rows, 256), 1) == source, got[:, :64]).astype(BF16)
    scales = jnp.sum(got[:, 64:].astype(F32), axis=1, keepdims=True)
    grafts = []
    for k in range(2):
        hit = iota((256, NB), 0) == table_ref[k + 1 : k + 2, 0:NB]
        grafts.append(whole_sum(jnp.where(hit, jnp.broadcast_to(scales, (256, NB)), 0.0)))
    graft_ref[...] = jnp.where(iota((1, 2), 1) == 0, grafts[0], grafts[1])


def per_device(gradient, second_moment, factors, old_owner, new_owner, offsets):
    old, own, off = (a.reshape(1, NB) for a in (old_owner, new_owner, offsets))
    grad, moment = gradient.reshape(4 * NB, 64), second_moment.reshape(4 * NB, 64)
    params = pltpu.CompilerParams(vmem_limit_bytes=40 * 1024 * 1024)
    wide_params = pltpu.CompilerParams(vmem_limit_bytes=60 * 1024 * 1024)
    index = pltpu.VMEM((1, NB), jnp.int32)
    with jax.named_scope("pack"):
        send = pl.pallas_call(
            pack_kernel,
            out_shape=jax.ShapeDtypeStruct((SENDROWS * NZ, 128), BF16),
            in_specs=[ANY] * 5,
            out_specs=VMEM,
            scratch_shapes=[
                pltpu.VMEM((4 * NB, 64), BF16),
                pltpu.VMEM((4 * NB, 64), F32),
                pltpu.VMEM((8 * NB, 64), BF16),
                index,
                index,
                pltpu.SemaphoreType.DMA((5,)),
            ],
            compiler_params=wide_params,
        )(grad, moment, factors.reshape(8 * NB, 64), old, off)
    with jax.named_scope("to_planes"):
        got = lax.all_to_all(send.reshape(NZ * SENDROWS // 2, 2, 128), "z", 0, 0, tiled=True)
    with jax.named_scope("spread"):
        send = pl.pallas_call(
            spread_kernel,
            out_shape=jax.ShapeDtypeStruct((16, 144, 128), BF16),
            in_specs=[VMEM],
            out_specs=VMEM,
            compiler_params=params,
        )(got.reshape(SENDROWS * NZ, 128))
    with jax.named_scope("in_plane"):
        got = lax.all_to_all(send, ("yh", "yl", "x"), 0, 0, tiled=True)
    with jax.named_scope("cores"):
        other = lax.ppermute(got, "c", [(0, 1), (1, 0)])
    with jax.named_scope("moment"):
        moment_new, table = pl.pallas_call(
            moment_kernel,
            out_shape=(
                jax.ShapeDtypeStruct((4 * NB, 64), F32),
                jax.ShapeDtypeStruct((8, 128), jnp.int32),
            ),
            in_specs=[ANY] * 6,
            out_specs=(VMEM, VMEM),
            scratch_shapes=[
                pltpu.VMEM((4 * NB, 64), BF16),
                pltpu.VMEM((4 * NB, 64), F32),
                index,
                index,
                index,
                pltpu.SemaphoreType.DMA((5,)),
            ],
            compiler_params=params,
        )(got, grad, moment, old, own, off)
    with jax.named_scope("block"):
        send = pl.pallas_call(
            block_kernel,
            out_shape=jax.ShapeDtypeStruct((256, 128), BF16),
            in_specs=[VMEM, VMEM, ANY],
            out_specs=VMEM,
            scratch_shapes=[pltpu.VMEM((512, 512), BF16)] * 2 + [pltpu.VMEM((8, 256, 128), BF16)],
            compiler_params=params,
        )(got, other, table)
    with jax.named_scope("back"):
        got = lax.all_to_all(send.reshape(64, 4, 128), ("yl", "z"), 0, 0, tiled=True)
    with jax.named_scope("unpack"):
        direction, grafts = pl.pallas_call(
            unpack_kernel,
            out_shape=(
                jax.ShapeDtypeStruct((4 * NB, 64), BF16),
                jax.ShapeDtypeStruct((1, 2), F32),
            ),
            in_specs=[VMEM, VMEM],
            out_specs=(VMEM, VMEM),
            compiler_params=params,
        )(table, got.reshape(256, 128))
    return (direction.reshape(NB, 4, 64), moment_new.reshape(NB, 4, 64), grafts)


def solution(mesh):
    split = Mesh(mesh.devices.reshape(2, 2, NZ, 4, 2), ("yh", "yl", "z", "x", "c"))
    dp, tensor = ("yh", "yl", "z"), ("x", "c")
    flat = P(None, dp, tensor)
    return jax.shard_map(
        per_device,
        mesh=split,
        in_specs=(flat, flat, P(None, None, dp, tensor), P(), P(), P()),
        out_specs=(flat, flat, P(dp, None)),
        check_vma=False,
    )
```

```python
import jax
import jax.numpy as jnp
from jax import lax
from jax.experimental import pallas as pl
from jax.experimental.pallas import tpu as pltpu
from jax.sharding import Mesh
from jax.sharding import PartitionSpec as P

BETA_TWO = 0.99
ADAM_EPS = 1e-08
NORM_EPS = 1e-06
F32 = jnp.float32
BF16 = jnp.bfloat16
NB = 56
NZ = 32
SENDROWS = 10
PLANE_FACTOR = 6554
FIRST = 20
ALONG_Z = [[(k + FIRST) % NZ for k in range(NZ)]]
ALONG_YZ = [[y * NZ + (k + FIRST) % NZ for y in range(2) for k in range(NZ)]]
VMEM = pl.BlockSpec(memory_space=pltpu.VMEM)
ANY = pl.BlockSpec(memory_space=pl.ANY)


def iota(shape, dim):
    return lax.broadcasted_iota(jnp.int32, shape, dim)


def total(mask, values, axis):
    picked = jnp.where(mask, values.astype(F32), 0.0)
    return jnp.sum(picked, axis=axis, keepdims=True).astype(jnp.int32)


def one_hot(mask):
    return jnp.where(mask, 1.0, 0.0).astype(BF16)


def pick(mask, rows):
    return jnp.dot(one_hot(mask), rows, preferred_element_type=F32)


def to_column(row):
    sub, lane = iota((NB, NB), 0), iota((NB, NB), 1)
    return total(sub == lane, jnp.broadcast_to(row, (NB, NB)), 1)


def to_column_wide(row):
    sub, lane = iota((NB, NB), 0), iota((NB, NB), 1)
    return jnp.sum(jnp.where(sub == lane, jnp.broadcast_to(row, (NB, NB)), 0.0), axis=1, keepdims=True)


def tied_before(row, column):
    sub, lane = iota((NB, NB), 0), iota((NB, NB), 1)
    return total((column == row) & (sub < lane), jnp.ones((NB, NB), jnp.int32), 0)


def slots_row(row, column):
    sub, lane = iota((NB, NB), 0), iota((NB, NB), 1)
    before = (column < row) | ((column == row) & (sub < lane))
    return total(before, jnp.ones((NB, NB), jnp.int32), 0)


def split_three(x):
    high = x.astype(BF16).astype(F32)
    rest = x - high
    mid = rest.astype(BF16).astype(F32)
    return high, mid, (rest - mid).astype(BF16).astype(F32)


def three_lanes(x, lane):
    high, mid, low = split_three(x)
    return jnp.where(lane == 0, high, jnp.where(lane == 1, mid, jnp.where(lane == 2, low, 0.0)))


def whole_sum(x):
    return jnp.sum(jnp.sum(x, axis=0, keepdims=True), axis=1, keepdims=True)


def adam_moment(grad, moment):
    wide = grad.astype(F32)
    return wide, BETA_TWO * moment + (1.0 - BETA_TWO) * wide * wide


def place(z):
    return (z + (NZ - FIRST)) & (NZ - 1)


def seat_row(slot):
    return ((slot & 1) * NZ + place(slot >> 1)) * 4


def dp_rank():
    return (lax.axis_index("yh") * 2 + lax.axis_index("yl")) * NZ + lax.axis_index("z")


def fetch(pairs, sems):
    copies = [pltpu.make_async_copy(src, dst, sems.at[i]) for i, (src, dst) in enumerate(pairs)]
    for copy in copies:
        copy.start()
    return copies


def pack_kernel(
    grad_hbm, moment_hbm, factor_hbm, old_hbm, off_hbm, send_ref,
    grad_ref, moment_ref, factor_ref, old_ref, off_ref, sems,
):
    copies = fetch(
        (
            (old_hbm, old_ref),
            (off_hbm, off_ref),
            (grad_hbm, grad_ref),
            (moment_hbm, moment_ref),
            (factor_hbm, factor_ref),
        ),
        sems,
    )
    row0 = dp_rank() * 4
    col0 = (lax.axis_index("x") * 2 + lax.axis_index("c")) * 64
    for copy in copies[:2]:
        copy.wait()
    old = old_ref[...]
    slot_col, off_col = to_column(slots_row(old, to_column(old))), to_column(off_ref[...])
    position = total(slot_col == iota((NB, NB), 1), jnp.broadcast_to(off_col, (NB, NB)), 0)
    rows = SENDROWS * NZ
    sent = iota((rows, NB), 0)
    group = (sent * PLANE_FACTOR) >> 16
    q = sent - SENDROWS * group
    plane = (group + FIRST) & (NZ - 1)
    seat = 2 * plane + ((q >> 2) & 1)
    spread = total(iota((rows, NB), 1) == seat, jnp.broadcast_to(position, (rows, NB)), 1)
    plane, q = plane[:, 0:1], q[:, 0:1]
    r = q & 3
    used = (q < 8) & (plane < NB // 2)
    from_factor = jnp.where(used, (2 * plane + (q >> 2)) * 8 + r, -1)
    from_grad = jnp.where(used, spread * 4 + r, jnp.where(q == 8, 4 * NB + plane, -9 * NB)) + 8 * NB
    k = iota((rows, 12 * NB + NZ), 1)
    mask = (k == from_factor) | (k == from_grad)
    for copy in copies[2:]:
        copy.wait()
    grad = grad_ref[...]
    wide, moment = adam_moment(grad, moment_ref[...])
    step = wide / (jnp.sqrt(moment) + ADAM_EPS)
    by_row = jnp.sum(step * step, axis=1, keepdims=True)
    mine = iota((4 * NB, NB), 1) == (iota((4 * NB, NB), 0) >> 2)
    by_block = jnp.sum(jnp.where(mine, by_row, 0.0), axis=0, keepdims=True)
    by_slot = jnp.sum(
        jnp.where(
            iota((NB, NB), 0) == jnp.broadcast_to(position, (NB, NB)), to_column_wide(by_block), 0.0
        ),
        axis=0,
        keepdims=True,
    )
    factor = factor_ref[...].astype(F32)
    r8, lane = iota((8 * NB, 64), 0) & 7, iota((8 * NB, 64), 1)
    row, col = row0 + (r8 & 3), col0 + lane
    right = pltpu.roll(factor, 8 * NB - 4, 0)
    mixed = jnp.where(col > row, factor, right)
    on_diagonal = jnp.sum(jnp.where((col == row) & (r8 < 4), factor, 0.0), axis=1, keepdims=True)
    r8, lane = iota((8 * NB, 128), 0), iota((8 * NB, 128), 1)
    seat_lane = 64 * ((r8 >> 3) & 1) + 8 + (r8 & 3)
    on_diagonal = jnp.where(lane == seat_lane, on_diagonal, 0.0).astype(BF16)
    extra = pick(iota((NZ, 8 * NB), 0) == (iota((NZ, 8 * NB), 1) >> 4), on_diagonal)
    p, s = iota((NZ, NB), 0), iota((NZ, NB), 1)
    for e in range(2):
        adam = jnp.sum(jnp.where(s == 2 * p + e, by_slot, 0.0), axis=1, keepdims=True)
        extra = extra + three_lanes(adam, iota((NZ, 128), 1) - 64 * e)
    none = jnp.zeros((8 * NB, 64), BF16)
    source = jnp.concatenate(
        [
            jnp.concatenate([mixed.astype(BF16), none], axis=1),
            jnp.concatenate([none[: 4 * NB], grad], axis=1),
            extra.astype(BF16),
        ],
        axis=0,
    )
    send_ref[...] = pick(mask, source).astype(BF16)


def moment_kernel(
    after_hbm, grad_hbm, moment_hbm, old_hbm, own_hbm, off_hbm, new_ref, table_ref,
    grad_ref, moment_ref, old_ref, own_ref, off_ref, sems,
):
    del after_hbm
    copies = fetch(
        (
            (old_hbm, old_ref),
            (off_hbm, off_ref),
            (own_hbm, own_ref),
            (grad_hbm, grad_ref),
            (moment_hbm, moment_ref),
        ),
        sems,
    )
    for copy in copies:
        copy.wait()
    new_ref[...] = adam_moment(grad_ref[...], moment_ref[...])[1]
    old, own = old_ref[...], own_ref[...]
    slot = slots_row(old, to_column(old))
    slot_col, off_col = to_column(slot), to_column(off_ref[...])
    at = total(off_col == iota((NB, NB), 1), jnp.broadcast_to(slot_col, (NB, NB)), 0)
    rank = tied_before(own, to_column(own))
    held = own == dp_rank()
    first_row = seat_row(slot)
    table_ref[0:1, 0:NB] = at
    for k in range(2):
        table_ref[k + 1 : k + 2, 0:NB] = jnp.where(held & (rank == k), first_row, -1)


def spread_kernel(in_ref, out_ref):
    n = SENDROWS * NZ
    got = in_ref[...]
    o, k = iota((256, n), 0), iota((256, n), 1)
    pairs = pick(k == place((o >> 2) & 31) * SENDROWS + (o >> 7) * 4 + (o & 3), got).astype(BF16)
    o, k = iota((NZ, n), 0), iota((NZ, n), 1)
    extra = pick(k == place(o) * SENDROWS + 8, got).astype(BF16)
    for e in range(2):
        lanes = slice(64 * e, 64 * e + 64)
        rest = jnp.concatenate([extra[:16, lanes], extra[16:, lanes]], axis=1)
        for dest in range(16):
            if (dest // 4) % 2 == e:
                out_ref[dest, 0:128] = pairs[128 * e : 128 * e + 128]
                out_ref[dest, 128:144] = rest


def block_kernel(own_ref, other_ref, table_hbm, out_ref, mixed, grad, parts):
    del table_hbm
    yh, x, c = lax.axis_index("yh"), lax.axis_index("x"), lax.axis_index("c")

    def assemble(low_ref, high_ref):
        for yy in range(4):
            for xx in range(4):
                i = yy * 4 + xx
                rr, cc = slice(128 * yy, 128 * yy + 128), slice(128 * xx, 128 * xx + 128)
                low, high = low_ref[i, 0:128, :], high_ref[i, 0:128, :]
                mixed[rr, cc] = jnp.concatenate([low[:, :64], high[:, :64]], axis=1)
                grad[rr, cc] = jnp.concatenate([low[:, 64:], high[:, 64:]], axis=1)

    @pl.when(c == 0)
    def _():
        assemble(own_ref, other_ref)

    @pl.when(c == 1)
    def _():
        assemble(other_ref, own_ref)

    extras = []
    for yy in range(4):
        parts_of = [ref[4 * yy + xx, 128:144, :].astype(F32) for ref in (own_ref, other_ref) for xx in range(4)]
        extras.append(sum(parts_of[1:], parts_of[0]))
    extra = jnp.concatenate(extras, axis=0)
    lane = iota((64, 128), 1) & 63
    adam_sq = whole_sum(jnp.where(lane < 3, extra, 0.0))
    diagonal = jnp.where(lane < 3, 0.0, extra).astype(BF16)
    i, k = iota((512, 64), 0), iota((512, 64), 1)
    diagonal = pick(k == ((i >> 7) * 16 + ((i >> 2) & 15)), diagonal)
    i, k = iota((512, 128), 0), iota((512, 128), 1)
    seat_lane = ((i >> 6) & 1) * 64 + 8 + (i & 3)
    diagonal = jnp.sum(jnp.where(k == seat_lane, diagonal, 0.0), axis=1, keepdims=True)
    entries = mixed[...].astype(F32)
    turned = entries.T
    row, col = iota((512, 512), 0), iota((512, 512), 1)
    left = jnp.where(col > row, entries, jnp.where(col < row, turned, diagonal)).astype(BF16)
    right = jnp.where(col > row, turned, entries).astype(BF16)
    lanes = (((1,), (1,)), ((), ()))
    product = lax.dot_general(right, grad[...], lanes, preferred_element_type=F32).astype(BF16)
    shampoo = lax.dot_general(left, product, lanes, preferred_element_type=F32).astype(BF16)
    wide = shampoo.astype(F32)
    scale = jnp.sqrt(adam_sq / (whole_sum(wide * wide) + NORM_EPS))
    direction = (scale * wide).astype(BF16)
    for hh in range(2):
        for xx in range(4):
            parts[4 * hh + xx] = direction[256 * hh : 256 * hh + 256, 128 * xx : 128 * xx + 128]
    mine = parts[4 * yh + x]
    mine = jnp.where(c == 0, mine[:, :64], mine[:, 64:])
    at = 4 * FIRST
    mine = jnp.concatenate([mine[at:128], mine[:at], mine[128 + at :], mine[128 : 128 + at]], axis=0)
    out_ref[...] = jnp.concatenate([mine, three_lanes(scale, iota((256, 64), 1)).astype(BF16)], axis=1)


def unpack_kernel(table_ref, in_ref, dir_ref, graft_ref):
    got = in_ref[...]
    rows = 4 * NB
    row = iota((rows, NB), 0)
    at = jnp.broadcast_to(table_ref[0:1, 0:NB], (rows, NB))
    s = total(iota((rows, NB), 1) == (row >> 2), at, 1)
    source = seat_row(s) + (iota((rows, 1), 0) & 3)
    dir_ref[...] = pick(iota((rows, 256), 1) == source, got[:, :64]).astype(BF16)
    scales = jnp.sum(got[:, 64:].astype(F32), axis=1, keepdims=True)
    grafts = []
    for k in range(2):
        hit = iota((256, NB), 0) == table_ref[k + 1 : k + 2, 0:NB]
        grafts.append(whole_sum(jnp.where(hit, jnp.broadcast_to(scales, (256, NB)), 0.0)))
    graft_ref[...] = jnp.where(iota((1, 2), 1) == 0, grafts[0], grafts[1])


def per_device(gradient, second_moment, factors, old_owner, new_owner, offsets):
    old, own, off = (a.reshape(1, NB) for a in (old_owner, new_owner, offsets))
    grad, moment = gradient.reshape(4 * NB, 64), second_moment.reshape(4 * NB, 64)
    params = pltpu.CompilerParams(vmem_limit_bytes=40 * 1024 * 1024)
    wide_params = pltpu.CompilerParams(vmem_limit_bytes=60 * 1024 * 1024)
    index = pltpu.VMEM((1, NB), jnp.int32)
    with jax.named_scope("pack"):
        send = pl.pallas_call(
            pack_kernel,
            out_shape=jax.ShapeDtypeStruct((SENDROWS * NZ, 128), BF16),
            in_specs=[ANY] * 5,
            out_specs=VMEM,
            scratch_shapes=[
                pltpu.VMEM((4 * NB, 64), BF16),
                pltpu.VMEM((4 * NB, 64), F32),
                pltpu.VMEM((8 * NB, 64), BF16),
                index,
                index,
                pltpu.SemaphoreType.DMA((5,)),
            ],
            compiler_params=wide_params,
        )(grad, moment, factors.reshape(8 * NB, 64), old, off)
    with jax.named_scope("to_planes"):
        got = lax.all_to_all(send.reshape(NZ * SENDROWS // 2, 2, 128), "z", 0, 0, tiled=True, axis_index_groups=ALONG_Z)
    with jax.named_scope("spread"):
        send = pl.pallas_call(
            spread_kernel,
            out_shape=jax.ShapeDtypeStruct((16, 144, 128), BF16),
            in_specs=[VMEM],
            out_specs=VMEM,
            compiler_params=params,
        )(got.reshape(SENDROWS * NZ, 128))
    with jax.named_scope("in_plane"):
        got = lax.all_to_all(send, ("yh", "yl", "x"), 0, 0, tiled=True)
    with jax.named_scope("cores"):
        other = lax.ppermute(got, "c", [(0, 1), (1, 0)])
    with jax.named_scope("moment"):
        moment_new, table = pl.pallas_call(
            moment_kernel,
            out_shape=(
                jax.ShapeDtypeStruct((4 * NB, 64), F32),
                jax.ShapeDtypeStruct((8, 128), jnp.int32),
            ),
            in_specs=[ANY] * 6,
            out_specs=(VMEM, VMEM),
            scratch_shapes=[
                pltpu.VMEM((4 * NB, 64), BF16),
                pltpu.VMEM((4 * NB, 64), F32),
                index,
                index,
                index,
                pltpu.SemaphoreType.DMA((5,)),
            ],
            compiler_params=params,
        )(got, grad, moment, old, own, off)
    with jax.named_scope("block"):
        send = pl.pallas_call(
            block_kernel,
            out_shape=jax.ShapeDtypeStruct((256, 128), BF16),
            in_specs=[VMEM, VMEM, ANY],
            out_specs=VMEM,
            scratch_shapes=[pltpu.VMEM((512, 512), BF16)] * 2 + [pltpu.VMEM((8, 256, 128), BF16)],
            compiler_params=params,
        )(got, other, table)
    with jax.named_scope("back"):
        got = lax.all_to_all(send.reshape(64, 4, 128), ("yl", "z"), 0, 0, tiled=True, axis_index_groups=ALONG_YZ)
    with jax.named_scope("unpack"):
        direction, grafts = pl.pallas_call(
            unpack_kernel,
            out_shape=(
                jax.ShapeDtypeStruct((4 * NB, 64), BF16),
                jax.ShapeDtypeStruct((1, 2), F32),
            ),
            in_specs=[VMEM, VMEM],
            out_specs=(VMEM, VMEM),
            compiler_params=params,
        )(table, got.reshape(256, 128))
    return (direction.reshape(NB, 4, 64), moment_new.reshape(NB, 4, 64), grafts)


def solution(mesh):
    split = Mesh(mesh.devices.reshape(2, 2, NZ, 4, 2), ("yh", "yl", "z", "x", "c"))
    dp, tensor = ("yh", "yl", "z"), ("x", "c")
    flat = P(None, dp, tensor)
    return jax.shard_map(
        per_device,
        mesh=split,
        in_specs=(flat, flat, P(None, None, dp, tensor), P(), P(), P()),
        out_specs=(flat, flat, P(dp, None)),
        check_vma=False,
    )
```

```python
import jax
import jax.numpy as jnp
from jax import lax
from jax.experimental import pallas as pl
from jax.experimental.pallas import tpu as pltpu
from jax.sharding import Mesh
from jax.sharding import PartitionSpec as P

BETA_TWO = 0.99
ADAM_EPS = 1e-08
NORM_EPS = 1e-06
F32 = jnp.float32
BF16 = jnp.bfloat16
NB = 56
NZ = 32
SENDROWS = 10
PLANE_FACTOR = 6554
FIRST = 22
FIRST_BACK = 18
LEAD = 10
IN_PLANE = [[(k + LEAD) % 16 for k in range(16)]]
ALONG_Z = [[(k + FIRST) % NZ for k in range(NZ)]]
ALONG_YZ = [[y * NZ + (k + FIRST_BACK) % NZ for y in range(2) for k in range(NZ)]]
VMEM = pl.BlockSpec(memory_space=pltpu.VMEM)
ANY = pl.BlockSpec(memory_space=pl.ANY)


def iota(shape, dim):
    return lax.broadcasted_iota(jnp.int32, shape, dim)


def total(mask, values, axis):
    picked = jnp.where(mask, values.astype(F32), 0.0)
    return jnp.sum(picked, axis=axis, keepdims=True).astype(jnp.int32)


def one_hot(mask):
    return jnp.where(mask, 1.0, 0.0).astype(BF16)


def pick(mask, rows):
    return jnp.dot(one_hot(mask), rows, preferred_element_type=F32)


def to_column(row):
    sub, lane = iota((NB, NB), 0), iota((NB, NB), 1)
    return total(sub == lane, jnp.broadcast_to(row, (NB, NB)), 1)


def to_column_wide(row):
    sub, lane = iota((NB, NB), 0), iota((NB, NB), 1)
    return jnp.sum(jnp.where(sub == lane, jnp.broadcast_to(row, (NB, NB)), 0.0), axis=1, keepdims=True)


def tied_before(row, column):
    sub, lane = iota((NB, NB), 0), iota((NB, NB), 1)
    return total((column == row) & (sub < lane), jnp.ones((NB, NB), jnp.int32), 0)


def slots_row(row, column):
    sub, lane = iota((NB, NB), 0), iota((NB, NB), 1)
    before = (column < row) | ((column == row) & (sub < lane))
    return total(before, jnp.ones((NB, NB), jnp.int32), 0)


def split_three(x):
    high = x.astype(BF16).astype(F32)
    rest = x - high
    mid = rest.astype(BF16).astype(F32)
    return high, mid, (rest - mid).astype(BF16).astype(F32)


def three_lanes(x, lane):
    high, mid, low = split_three(x)
    return jnp.where(lane == 0, high, jnp.where(lane == 1, mid, jnp.where(lane == 2, low, 0.0)))


def whole_sum(x):
    return jnp.sum(jnp.sum(x, axis=0, keepdims=True), axis=1, keepdims=True)


def adam_moment(grad, moment):
    wide = grad.astype(F32)
    return wide, BETA_TWO * moment + (1.0 - BETA_TWO) * wide * wide


def place(z, first):
    return (z + (NZ - first)) & (NZ - 1)


def seat_row(slot):
    return ((slot & 1) * NZ + place(slot >> 1, FIRST_BACK)) * 4


def dp_rank():
    return (lax.axis_index("yh") * 2 + lax.axis_index("yl")) * NZ + lax.axis_index("z")


def fetch(pairs, sems):
    copies = [pltpu.make_async_copy(src, dst, sems.at[i]) for i, (src, dst) in enumerate(pairs)]
    for copy in copies:
        copy.start()
    return copies


def pack_kernel(
    grad_hbm, moment_hbm, factor_hbm, old_hbm, off_hbm, send_ref,
    grad_ref, moment_ref, factor_ref, old_ref, off_ref, sems,
):
    copies = fetch(
        (
            (old_hbm, old_ref),
            (off_hbm, off_ref),
            (grad_hbm, grad_ref),
            (moment_hbm, moment_ref),
            (factor_hbm, factor_ref),
        ),
        sems,
    )
    row0 = dp_rank() * 4
    col0 = (lax.axis_index("x") * 2 + lax.axis_index("c")) * 64
    for copy in copies[:2]:
        copy.wait()
    old = old_ref[...]
    slot_col, off_col = to_column(slots_row(old, to_column(old))), to_column(off_ref[...])
    position = total(slot_col == iota((NB, NB), 1), jnp.broadcast_to(off_col, (NB, NB)), 0)
    rows = SENDROWS * NZ
    sent = iota((rows, NB), 0)
    group = (sent * PLANE_FACTOR) >> 16
    q = sent - SENDROWS * group
    plane = (group + FIRST) & (NZ - 1)
    seat = 2 * plane + ((q >> 2) & 1)
    spread = total(iota((rows, NB), 1) == seat, jnp.broadcast_to(position, (rows, NB)), 1)
    plane, q = plane[:, 0:1], q[:, 0:1]
    r = q & 3
    used = (q < 8) & (plane < NB // 2)
    from_factor = jnp.where(used, (2 * plane + (q >> 2)) * 8 + r, -1)
    from_grad = jnp.where(used, spread * 4 + r, jnp.where(q == 8, 4 * NB + plane, -9 * NB)) + 8 * NB
    k = iota((rows, 12 * NB + NZ), 1)
    mask = (k == from_factor) | (k == from_grad)
    for copy in copies[2:]:
        copy.wait()
    grad = grad_ref[...]
    wide, moment = adam_moment(grad, moment_ref[...])
    step = wide / (jnp.sqrt(moment) + ADAM_EPS)
    by_row = jnp.sum(step * step, axis=1, keepdims=True)
    mine = iota((4 * NB, NB), 1) == (iota((4 * NB, NB), 0) >> 2)
    by_block = jnp.sum(jnp.where(mine, by_row, 0.0), axis=0, keepdims=True)
    by_slot = jnp.sum(
        jnp.where(
            iota((NB, NB), 0) == jnp.broadcast_to(position, (NB, NB)), to_column_wide(by_block), 0.0
        ),
        axis=0,
        keepdims=True,
    )
    factor = factor_ref[...].astype(F32)
    r8, lane = iota((8 * NB, 64), 0) & 7, iota((8 * NB, 64), 1)
    row, col = row0 + (r8 & 3), col0 + lane
    right = pltpu.roll(factor, 8 * NB - 4, 0)
    mixed = jnp.where(col > row, factor, right)
    on_diagonal = jnp.sum(jnp.where((col == row) & (r8 < 4), factor, 0.0), axis=1, keepdims=True)
    r8, lane = iota((8 * NB, 128), 0), iota((8 * NB, 128), 1)
    seat_lane = 64 * ((r8 >> 3) & 1) + 8 + (r8 & 3)
    on_diagonal = jnp.where(lane == seat_lane, on_diagonal, 0.0).astype(BF16)
    extra = pick(iota((NZ, 8 * NB), 0) == (iota((NZ, 8 * NB), 1) >> 4), on_diagonal)
    p, s = iota((NZ, NB), 0), iota((NZ, NB), 1)
    for e in range(2):
        adam = jnp.sum(jnp.where(s == 2 * p + e, by_slot, 0.0), axis=1, keepdims=True)
        extra = extra + three_lanes(adam, iota((NZ, 128), 1) - 64 * e)
    none = jnp.zeros((8 * NB, 64), BF16)
    source = jnp.concatenate(
        [
            jnp.concatenate([mixed.astype(BF16), none], axis=1),
            jnp.concatenate([none[: 4 * NB], grad], axis=1),
            extra.astype(BF16),
        ],
        axis=0,
    )
    send_ref[...] = pick(mask, source).astype(BF16)


def moment_kernel(
    after_hbm, grad_hbm, moment_hbm, old_hbm, own_hbm, off_hbm, new_ref, table_ref,
    grad_ref, moment_ref, old_ref, own_ref, off_ref, sems,
):
    del after_hbm
    copies = fetch(
        (
            (old_hbm, old_ref),
            (off_hbm, off_ref),
            (own_hbm, own_ref),
            (grad_hbm, grad_ref),
            (moment_hbm, moment_ref),
        ),
        sems,
    )
    for copy in copies:
        copy.wait()
    new_ref[...] = adam_moment(grad_ref[...], moment_ref[...])[1]
    old, own = old_ref[...], own_ref[...]
    slot = slots_row(old, to_column(old))
    slot_col, off_col = to_column(slot), to_column(off_ref[...])
    at = total(off_col == iota((NB, NB), 1), jnp.broadcast_to(slot_col, (NB, NB)), 0)
    rank = tied_before(own, to_column(own))
    held = own == dp_rank()
    first_row = seat_row(slot)
    table_ref[0:1, 0:NB] = at
    for k in range(2):
        table_ref[k + 1 : k + 2, 0:NB] = jnp.where(held & (rank == k), first_row, -1)


def spread_kernel(in_ref, out_ref):
    n = SENDROWS * NZ
    got = in_ref[...]
    o, k = iota((256, n), 0), iota((256, n), 1)
    pairs = pick(k == place((o >> 2) & 31, FIRST) * SENDROWS + (o >> 7) * 4 + (o & 3), got).astype(BF16)
    o, k = iota((NZ, n), 0), iota((NZ, n), 1)
    extra = pick(k == place(o, FIRST) * SENDROWS + 8, got).astype(BF16)
    for e in range(2):
        lanes = slice(64 * e, 64 * e + 64)
        rest = jnp.concatenate([extra[:16, lanes], extra[16:, lanes]], axis=1)
        for dest in range(16):
            if (dest // 4) % 2 == e:
                out_ref[(dest - LEAD) % 16, 0:128] = pairs[128 * e : 128 * e + 128]
                out_ref[(dest - LEAD) % 16, 128:144] = rest


def block_kernel(own_ref, other_ref, table_hbm, out_ref, mixed, grad, parts):
    del table_hbm
    yh, x, c = lax.axis_index("yh"), lax.axis_index("x"), lax.axis_index("c")

    def assemble(low_ref, high_ref):
        for yy in range(4):
            for xx in range(4):
                i = (yy * 4 + xx - LEAD) % 16
                rr, cc = slice(128 * yy, 128 * yy + 128), slice(128 * xx, 128 * xx + 128)
                low, high = low_ref[i, 0:128, :], high_ref[i, 0:128, :]
                mixed[rr, cc] = jnp.concatenate([low[:, :64], high[:, :64]], axis=1)
                grad[rr, cc] = jnp.concatenate([low[:, 64:], high[:, 64:]], axis=1)

    @pl.when(c == 0)
    def _():
        assemble(own_ref, other_ref)

    @pl.when(c == 1)
    def _():
        assemble(other_ref, own_ref)

    extras = []
    for yy in range(4):
        parts_of = [
            ref[(4 * yy + xx - LEAD) % 16, 128:144, :].astype(F32)
            for ref in (own_ref, other_ref)
            for xx in range(4)
        ]
        extras.append(sum(parts_of[1:], parts_of[0]))
    extra = jnp.concatenate(extras, axis=0)
    lane = iota((64, 128), 1) & 63
    adam_sq = whole_sum(jnp.where(lane < 3, extra, 0.0))
    diagonal = jnp.where(lane < 3, 0.0, extra).astype(BF16)
    i, k = iota((512, 64), 0), iota((512, 64), 1)
    diagonal = pick(k == ((i >> 7) * 16 + ((i >> 2) & 15)), diagonal)
    i, k = iota((512, 128), 0), iota((512, 128), 1)
    seat_lane = ((i >> 6) & 1) * 64 + 8 + (i & 3)
    diagonal = jnp.sum(jnp.where(k == seat_lane, diagonal, 0.0), axis=1, keepdims=True)
    entries = mixed[...].astype(F32)
    turned = entries.T
    row, col = iota((512, 512), 0), iota((512, 512), 1)
    left = jnp.where(col > row, entries, jnp.where(col < row, turned, diagonal)).astype(BF16)
    right = jnp.where(col > row, turned, entries).astype(BF16)
    lanes = (((1,), (1,)), ((), ()))
    product = lax.dot_general(right, grad[...], lanes, preferred_element_type=F32).astype(BF16)
    shampoo = lax.dot_general(left, product, lanes, preferred_element_type=F32).astype(BF16)
    wide = shampoo.astype(F32)
    scale = jnp.sqrt(adam_sq / (whole_sum(wide * wide) + NORM_EPS))
    direction = scale * wide
    at = 4 * FIRST_BACK
    for hh in range(2):
        ends = []
        for row in (256 * hh, 256 * hh + 128):
            ends += [direction[row + at : row + 128], direction[row : row + at]]
        rows = jnp.concatenate(ends, axis=0).astype(BF16)
        for xx in range(4):
            parts[4 * hh + xx] = rows[:, 128 * xx : 128 * xx + 128]
    mine = parts[4 * yh + x]
    mine = jnp.where(c == 0, mine[:, :64], mine[:, 64:])
    out_ref[...] = jnp.concatenate([mine, three_lanes(scale, iota((256, 64), 1)).astype(BF16)], axis=1)


def unpack_kernel(table_ref, in_ref, dir_ref, graft_ref):
    got = in_ref[...]
    rows = 4 * NB
    row = iota((rows, NB), 0)
    at = jnp.broadcast_to(table_ref[0:1, 0:NB], (rows, NB))
    s = total(iota((rows, NB), 1) == (row >> 2), at, 1)
    source = seat_row(s) + (iota((rows, 1), 0) & 3)
    dir_ref[...] = pick(iota((rows, 256), 1) == source, got[:, :64]).astype(BF16)
    scales = jnp.sum(got[:, 64:].astype(F32), axis=1, keepdims=True)
    grafts = []
    for k in range(2):
        hit = iota((256, NB), 0) == table_ref[k + 1 : k + 2, 0:NB]
        grafts.append(whole_sum(jnp.where(hit, jnp.broadcast_to(scales, (256, NB)), 0.0)))
    graft_ref[...] = jnp.where(iota((1, 2), 1) == 0, grafts[0], grafts[1])


def in_hbm(x):
    return pltpu.with_memory_space_constraint(x, pltpu.HBM)


def per_device(gradient, second_moment, factors, old_owner, new_owner, offsets):
    old, own, off = (a.reshape(1, NB) for a in (old_owner, new_owner, offsets))
    grad, moment = gradient.reshape(4 * NB, 64), second_moment.reshape(4 * NB, 64)
    params = pltpu.CompilerParams(vmem_limit_bytes=40 * 1024 * 1024)
    wide_params = pltpu.CompilerParams(vmem_limit_bytes=60 * 1024 * 1024)
    index = pltpu.VMEM((1, NB), jnp.int32)
    with jax.named_scope("pack"):
        send = pl.pallas_call(
            pack_kernel,
            out_shape=jax.ShapeDtypeStruct((SENDROWS * NZ, 128), BF16),
            in_specs=[ANY] * 5,
            out_specs=VMEM,
            scratch_shapes=[
                pltpu.VMEM((4 * NB, 64), BF16),
                pltpu.VMEM((4 * NB, 64), F32),
                pltpu.VMEM((8 * NB, 64), BF16),
                index,
                index,
                pltpu.SemaphoreType.DMA((5,)),
            ],
            compiler_params=params,
        )(*(in_hbm(a) for a in (grad, moment, factors.reshape(8 * NB, 64), old, off)))
    with jax.named_scope("to_planes"):
        got = lax.all_to_all(send.reshape(NZ * SENDROWS // 2, 2, 128), "z", 0, 0, tiled=True, axis_index_groups=ALONG_Z)
    with jax.named_scope("spread"):
        send = pl.pallas_call(
            spread_kernel,
            out_shape=jax.ShapeDtypeStruct((16, 144, 128), BF16),
            in_specs=[VMEM],
            out_specs=VMEM,
            compiler_params=params,
        )(got.reshape(SENDROWS * NZ, 128))
    with jax.named_scope("in_plane"):
        got = lax.all_to_all(send, ("yh", "yl", "x"), 0, 0, tiled=True, axis_index_groups=IN_PLANE)
    with jax.named_scope("cores"):
        other = lax.ppermute(got, "c", [(0, 1), (1, 0)])
    with jax.named_scope("moment"):
        moment_new, table = pl.pallas_call(
            moment_kernel,
            out_shape=(
                jax.ShapeDtypeStruct((4 * NB, 64), F32),
                jax.ShapeDtypeStruct((8, 128), jnp.int32),
            ),
            in_specs=[ANY] * 6,
            out_specs=(VMEM, VMEM),
            scratch_shapes=[
                pltpu.VMEM((4 * NB, 64), BF16),
                pltpu.VMEM((4 * NB, 64), F32),
                index,
                index,
                index,
                pltpu.SemaphoreType.DMA((5,)),
            ],
            compiler_params=params,
        )(got, grad, moment, old, own, off)
    with jax.named_scope("block"):
        send = pl.pallas_call(
            block_kernel,
            out_shape=jax.ShapeDtypeStruct((256, 128), BF16),
            in_specs=[VMEM, VMEM, ANY],
            out_specs=VMEM,
            scratch_shapes=[pltpu.VMEM((512, 512), BF16)] * 2 + [pltpu.VMEM((8, 256, 128), BF16)],
            compiler_params=params,
        )(got, other, table)
    with jax.named_scope("back"):
        got = lax.all_to_all(send.reshape(64, 4, 128), ("yl", "z"), 0, 0, tiled=True, axis_index_groups=ALONG_YZ)
    with jax.named_scope("unpack"):
        direction, grafts = pl.pallas_call(
            unpack_kernel,
            out_shape=(
                jax.ShapeDtypeStruct((4 * NB, 64), BF16),
                jax.ShapeDtypeStruct((1, 2), F32),
            ),
            in_specs=[VMEM, VMEM],
            out_specs=(VMEM, VMEM),
            compiler_params=params,
        )(table, got.reshape(256, 128))
    return (direction.reshape(NB, 4, 64), moment_new.reshape(NB, 4, 64), grafts)


def solution(mesh):
    split = Mesh(mesh.devices.reshape(2, 2, NZ, 4, 2), ("yh", "yl", "z", "x", "c"))
    dp, tensor = ("yh", "yl", "z"), ("x", "c")
    flat = P(None, dp, tensor)
    return jax.shard_map(
        per_device,
        mesh=split,
        in_specs=(flat, flat, P(None, None, dp, tensor), P(), P(), P()),
        out_specs=(flat, flat, P(dp, None)),
        check_vma=False,
    )
```

```python
import jax
import jax.numpy as jnp
from jax import lax
from jax.experimental import pallas as pl
from jax.experimental.pallas import tpu as pltpu
from jax.sharding import Mesh
from jax.sharding import PartitionSpec as P

BETA_TWO = 0.99
ADAM_EPS = 1e-08
NORM_EPS = 1e-06
F32 = jnp.float32
BF16 = jnp.bfloat16
NB = 56
NZ = 32
SENDROWS = 10
FIRST = 22
FIRST_BACK = 18
LEAD = 10
IN_PLANE = [[(k + LEAD) % 16 for k in range(16)]]
ALONG_Z = [[(k + FIRST) % NZ for k in range(NZ)]]
ALONG_YZ = [[y * NZ + (k + FIRST_BACK) % NZ for y in range(2) for k in range(NZ)]]
VMEM = pl.BlockSpec(memory_space=pltpu.VMEM)
ANY = pl.BlockSpec(memory_space=pl.ANY)


def iota(shape, dim):
    return lax.broadcasted_iota(jnp.int32, shape, dim)


def total(mask, values, axis):
    picked = jnp.where(mask, values.astype(F32), 0.0)
    return jnp.sum(picked, axis=axis, keepdims=True).astype(jnp.int32)


def one_hot(mask):
    return jnp.where(mask, 1.0, 0.0).astype(BF16)


def pick(mask, rows):
    return jnp.dot(one_hot(mask), rows, preferred_element_type=F32)


def to_column(row):
    sub, lane = iota((NB, NB), 0), iota((NB, NB), 1)
    return total(sub == lane, jnp.broadcast_to(row, (NB, NB)), 1)


def to_column_wide(row):
    sub, lane = iota((NB, NB), 0), iota((NB, NB), 1)
    return jnp.sum(jnp.where(sub == lane, jnp.broadcast_to(row, (NB, NB)), 0.0), axis=1, keepdims=True)


def tied_before(row, column):
    sub, lane = iota((NB, NB), 0), iota((NB, NB), 1)
    return total((column == row) & (sub < lane), jnp.ones((NB, NB), jnp.int32), 0)


def slots_row(row, column):
    sub, lane = iota((NB, NB), 0), iota((NB, NB), 1)
    before = (column < row) | ((column == row) & (sub < lane))
    return total(before, jnp.ones((NB, NB), jnp.int32), 0)


def split_three(x):
    high = x.astype(BF16).astype(F32)
    rest = x - high
    mid = rest.astype(BF16).astype(F32)
    return high, mid, (rest - mid).astype(BF16).astype(F32)


def three_lanes(x, lane):
    high, mid, low = split_three(x)
    return jnp.where(lane == 0, high, jnp.where(lane == 1, mid, jnp.where(lane == 2, low, 0.0)))


def whole_sum(x):
    return jnp.sum(jnp.sum(x, axis=0, keepdims=True), axis=1, keepdims=True)


def adam_moment(grad, moment):
    wide = grad.astype(F32)
    return wide, BETA_TWO * moment + (1.0 - BETA_TWO) * wide * wide


def place(z, first):
    return (z + (NZ - first)) & (NZ - 1)


def seat_row(slot):
    return ((slot & 1) * NZ + place(slot >> 1, FIRST_BACK)) * 4


def dp_rank():
    return (lax.axis_index("yh") * 2 + lax.axis_index("yl")) * NZ + lax.axis_index("z")


def fetch(pairs, sems):
    copies = [pltpu.make_async_copy(src, dst, sems.at[i]) for i, (src, dst) in enumerate(pairs)]
    for copy in copies:
        copy.start()
    return copies


def pack_kernel(
    grad_hbm, moment_hbm, factor_hbm, old_hbm, off_hbm, send_ref,
    grad_ref, moment_ref, factor_ref, old_ref, off_ref, stage, sems,
):
    copies = fetch(
        (
            (old_hbm, old_ref),
            (off_hbm, off_ref),
            (grad_hbm, grad_ref),
            (moment_hbm, moment_ref),
            (factor_hbm, factor_ref),
        ),
        sems,
    )
    row0 = dp_rank() * 4
    col0 = (lax.axis_index("x") * 2 + lax.axis_index("c")) * 64
    stage[...] = jnp.zeros((SENDROWS * NZ, 128), F32)
    for copy in copies:
        copy.wait()
    old = old_ref[...]
    slot_col, off_col = to_column(slots_row(old, to_column(old))), to_column(off_ref[...])
    position = total(slot_col == iota((NB, NB), 1), jnp.broadcast_to(off_col, (NB, NB)), 0)
    rows = 4 * NB
    spread = total(
        iota((rows, NB), 1) == (iota((rows, NB), 0) >> 2),
        jnp.broadcast_to(position, (rows, NB)),
        1,
    )
    source = spread * 4 + (iota((rows, 1), 0) & 3)
    grad = grad_ref[...]
    mine = pick(iota((rows, rows), 1) == source, grad)
    wide, moment = adam_moment(grad, moment_ref[...])
    step = wide / (jnp.sqrt(moment) + ADAM_EPS)
    by_row = jnp.sum(step * step, axis=1, keepdims=True)
    of_block = iota((rows, NB), 1) == (iota((rows, NB), 0) >> 2)
    by_block = jnp.sum(jnp.where(of_block, by_row, 0.0), axis=0, keepdims=True)
    by_slot = jnp.sum(
        jnp.where(
            iota((NB, NB), 0) == jnp.broadcast_to(position, (NB, NB)), to_column_wide(by_block), 0.0
        ),
        axis=0,
        keepdims=True,
    )
    planes = NB // 2
    factor = factor_ref[...].astype(F32).reshape(planes, 2, 8, 64)
    first, second = factor[:, 0], factor[:, 1]
    shape = (planes, 8, 64)
    sub, lane = iota(shape, 1), iota(shape, 2)
    row, col = row0 + (sub & 3), col0 + lane
    left = jnp.where(sub < 4, first, pltpu.roll(second, 4, 1))
    right = jnp.where(sub < 4, pltpu.roll(first, 4, 1), second)
    mixed = jnp.where(col > row, left, right).reshape(rows, 64)
    on_diagonal = jnp.sum(jnp.where(col == row, left, 0.0), axis=2, keepdims=True)
    shape = (planes, 8, 128)
    sub, lane = iota(shape, 1), iota(shape, 2)
    seat_lane = 64 * (sub >> 2) + 8 + (sub & 3)
    on_diagonal = jnp.sum(jnp.where(lane == seat_lane, on_diagonal, 0.0), axis=1, keepdims=True)
    extra = jnp.zeros((NZ, 128), F32)
    p, s = iota((NZ, NB), 0), iota((NZ, NB), 1)
    for e in range(2):
        adam = jnp.sum(jnp.where(s == 2 * p + e, by_slot, 0.0), axis=1, keepdims=True)
        extra = extra + three_lanes(adam, iota((NZ, 128), 1) - 64 * e)
    both = jnp.concatenate([mixed, mine], axis=1)
    for plane in range(planes):
        at = SENDROWS * ((plane - FIRST) % NZ)
        stage[at : at + 8, :] = both[8 * plane : 8 * plane + 8]
        stage[at + 8 : at + 9, :] = extra[plane : plane + 1] + on_diagonal[plane]
    send_ref[...] = stage[...].astype(BF16)


def moment_kernel(
    after_hbm, grad_hbm, moment_hbm, old_hbm, own_hbm, off_hbm, new_ref, table_ref,
    grad_ref, moment_ref, old_ref, own_ref, off_ref, sems,
):
    del after_hbm
    copies = fetch(
        (
            (old_hbm, old_ref),
            (off_hbm, off_ref),
            (own_hbm, own_ref),
            (grad_hbm, grad_ref),
            (moment_hbm, moment_ref),
        ),
        sems,
    )
    for copy in copies:
        copy.wait()
    new_ref[...] = adam_moment(grad_ref[...], moment_ref[...])[1]
    old, own = old_ref[...], own_ref[...]
    slot = slots_row(old, to_column(old))
    slot_col, off_col = to_column(slot), to_column(off_ref[...])
    at = total(off_col == iota((NB, NB), 1), jnp.broadcast_to(slot_col, (NB, NB)), 0)
    rank = tied_before(own, to_column(own))
    held = own == dp_rank()
    first_row = seat_row(slot)
    table_ref[0:1, 0:NB] = at
    for k in range(2):
        table_ref[k + 1 : k + 2, 0:NB] = jnp.where(held & (rank == k), first_row, -1)


def spread_kernel(in_ref, out_ref):
    n = SENDROWS * NZ
    got = in_ref[...]
    o, k = iota((256, n), 0), iota((256, n), 1)
    pairs = pick(k == place((o >> 2) & 31, FIRST) * SENDROWS + (o >> 7) * 4 + (o & 3), got).astype(BF16)
    o, k = iota((NZ, n), 0), iota((NZ, n), 1)
    extra = pick(k == place(o, FIRST) * SENDROWS + 8, got).astype(BF16)
    for e in range(2):
        lanes = slice(64 * e, 64 * e + 64)
        rest = jnp.concatenate([extra[:16, lanes], extra[16:, lanes]], axis=1)
        for dest in range(16):
            if (dest // 4) % 2 == e:
                out_ref[(dest - LEAD) % 16, 0:128] = pairs[128 * e : 128 * e + 128]
                out_ref[(dest - LEAD) % 16, 128:144] = rest


def block_kernel(own_ref, other_ref, table_hbm, out_ref, mixed, grad, parts):
    del table_hbm
    yh, x, c = lax.axis_index("yh"), lax.axis_index("x"), lax.axis_index("c")

    def assemble(low_ref, high_ref):
        for yy in range(4):
            for xx in range(4):
                i = (yy * 4 + xx - LEAD) % 16
                rr, cc = slice(128 * yy, 128 * yy + 128), slice(128 * xx, 128 * xx + 128)
                low, high = low_ref[i, 0:128, :], high_ref[i, 0:128, :]
                mixed[rr, cc] = jnp.concatenate([low[:, :64], high[:, :64]], axis=1)
                grad[rr, cc] = jnp.concatenate([low[:, 64:], high[:, 64:]], axis=1)

    @pl.when(c == 0)
    def _():
        assemble(own_ref, other_ref)

    @pl.when(c == 1)
    def _():
        assemble(other_ref, own_ref)

    extras = []
    for yy in range(4):
        parts_of = [
            ref[(4 * yy + xx - LEAD) % 16, 128:144, :].astype(F32)
            for ref in (own_ref, other_ref)
            for xx in range(4)
        ]
        extras.append(sum(parts_of[1:], parts_of[0]))
    extra = jnp.concatenate(extras, axis=0)
    lane = iota((64, 128), 1) & 63
    adam_sq = whole_sum(jnp.where(lane < 3, extra, 0.0))
    diagonal = jnp.where(lane < 3, 0.0, extra).astype(BF16)
    i, k = iota((512, 64), 0), iota((512, 64), 1)
    diagonal = pick(k == ((i >> 7) * 16 + ((i >> 2) & 15)), diagonal)
    i, k = iota((512, 128), 0), iota((512, 128), 1)
    seat_lane = ((i >> 6) & 1) * 64 + 8 + (i & 3)
    diagonal = jnp.sum(jnp.where(k == seat_lane, diagonal, 0.0), axis=1, keepdims=True)
    entries = mixed[...].astype(F32)
    turned = entries.T
    row, col = iota((512, 512), 0), iota((512, 512), 1)
    left = jnp.where(col > row, entries, jnp.where(col < row, turned, diagonal)).astype(BF16)
    right = jnp.where(col > row, turned, entries).astype(BF16)
    lanes = (((1,), (1,)), ((), ()))
    product = lax.dot_general(right, grad[...], lanes, preferred_element_type=F32).astype(BF16)
    shampoo = lax.dot_general(left, product, lanes, preferred_element_type=F32).astype(BF16)
    wide = shampoo.astype(F32)
    scale = jnp.sqrt(adam_sq / (whole_sum(wide * wide) + NORM_EPS))
    for hh in range(2):
        for xx in range(4):
            parts[4 * hh + xx] = shampoo[256 * hh : 256 * hh + 256, 128 * xx : 128 * xx + 128]
    mine = scale * parts[4 * yh + x].astype(F32)
    mine = jnp.where(c == 0, mine[:, :64], mine[:, 64:])
    at = 4 * FIRST_BACK
    mine = jnp.concatenate([mine[at:128], mine[:at], mine[128 + at :], mine[128 : 128 + at]], axis=0)
    mine = mine.astype(BF16)
    out_ref[...] = jnp.concatenate([mine, three_lanes(scale, iota((256, 64), 1)).astype(BF16)], axis=1)


def unpack_kernel(table_ref, in_ref, dir_ref, graft_ref):
    got = in_ref[...]
    rows = 4 * NB
    row = iota((rows, NB), 0)
    at = jnp.broadcast_to(table_ref[0:1, 0:NB], (rows, NB))
    s = total(iota((rows, NB), 1) == (row >> 2), at, 1)
    source = seat_row(s) + (iota((rows, 1), 0) & 3)
    dir_ref[...] = pick(iota((rows, 256), 1) == source, got[:, :64]).astype(BF16)
    scales = jnp.sum(got[:, 64:].astype(F32), axis=1, keepdims=True)
    grafts = []
    for k in range(2):
        hit = iota((256, NB), 0) == table_ref[k + 1 : k + 2, 0:NB]
        grafts.append(whole_sum(jnp.where(hit, jnp.broadcast_to(scales, (256, NB)), 0.0)))
    graft_ref[...] = jnp.where(iota((1, 2), 1) == 0, grafts[0], grafts[1])


def in_hbm(x):
    return pltpu.with_memory_space_constraint(x, pltpu.HBM)


def per_device(gradient, second_moment, factors, old_owner, new_owner, offsets):
    old, own, off = (a.reshape(1, NB) for a in (old_owner, new_owner, offsets))
    grad, moment = gradient.reshape(4 * NB, 64), second_moment.reshape(4 * NB, 64)
    params = pltpu.CompilerParams(vmem_limit_bytes=40 * 1024 * 1024)
    index = pltpu.VMEM((1, NB), jnp.int32)
    with jax.named_scope("pack"):
        send = pl.pallas_call(
            pack_kernel,
            out_shape=jax.ShapeDtypeStruct((SENDROWS * NZ, 128), BF16),
            in_specs=[ANY] * 5,
            out_specs=VMEM,
            scratch_shapes=[
                pltpu.VMEM((4 * NB, 64), BF16),
                pltpu.VMEM((4 * NB, 64), F32),
                pltpu.VMEM((8 * NB, 64), BF16),
                index,
                index,
                pltpu.VMEM((SENDROWS * NZ, 128), F32),
                pltpu.SemaphoreType.DMA((5,)),
            ],
            compiler_params=params,
        )(*(in_hbm(a) for a in (grad, moment, factors.reshape(8 * NB, 64), old, off)))
    with jax.named_scope("to_planes"):
        got = lax.all_to_all(send.reshape(NZ * SENDROWS // 2, 2, 128), "z", 0, 0, tiled=True, axis_index_groups=ALONG_Z)
    with jax.named_scope("spread"):
        send = pl.pallas_call(
            spread_kernel,
            out_shape=jax.ShapeDtypeStruct((16, 144, 128), BF16),
            in_specs=[VMEM],
            out_specs=VMEM,
            compiler_params=params,
        )(got.reshape(SENDROWS * NZ, 128))
    with jax.named_scope("in_plane"):
        got = lax.all_to_all(send, ("yh", "yl", "x"), 0, 0, tiled=True, axis_index_groups=IN_PLANE)
    with jax.named_scope("cores"):
        other = lax.ppermute(got, "c", [(0, 1), (1, 0)])
    with jax.named_scope("moment"):
        moment_new, table = pl.pallas_call(
            moment_kernel,
            out_shape=(
                jax.ShapeDtypeStruct((4 * NB, 64), F32),
                jax.ShapeDtypeStruct((8, 128), jnp.int32),
            ),
            in_specs=[ANY] * 6,
            out_specs=(VMEM, VMEM),
            scratch_shapes=[
                pltpu.VMEM((4 * NB, 64), BF16),
                pltpu.VMEM((4 * NB, 64), F32),
                index,
                index,
                index,
                pltpu.SemaphoreType.DMA((5,)),
            ],
            compiler_params=params,
        )(got, grad, moment, old, own, off)
    with jax.named_scope("block"):
        send = pl.pallas_call(
            block_kernel,
            out_shape=jax.ShapeDtypeStruct((256, 128), BF16),
            in_specs=[VMEM, VMEM, ANY],
            out_specs=VMEM,
            scratch_shapes=[pltpu.VMEM((512, 512), BF16)] * 2 + [pltpu.VMEM((8, 256, 128), BF16)],
            compiler_params=params,
        )(got, other, table)
    with jax.named_scope("back"):
        got = lax.all_to_all(send.reshape(64, 4, 128), ("yl", "z"), 0, 0, tiled=True, axis_index_groups=ALONG_YZ)
    with jax.named_scope("unpack"):
        direction, grafts = pl.pallas_call(
            unpack_kernel,
            out_shape=(
                jax.ShapeDtypeStruct((4 * NB, 64), BF16),
                jax.ShapeDtypeStruct((1, 2), F32),
            ),
            in_specs=[VMEM, VMEM],
            out_specs=(VMEM, VMEM),
            compiler_params=params,
        )(table, got.reshape(256, 128))
    return (direction.reshape(NB, 4, 64), moment_new.reshape(NB, 4, 64), grafts)


def solution(mesh):
    split = Mesh(mesh.devices.reshape(2, 2, NZ, 4, 2), ("yh", "yl", "z", "x", "c"))
    dp, tensor = ("yh", "yl", "z"), ("x", "c")
    flat = P(None, dp, tensor)
    return jax.shard_map(
        per_device,
        mesh=split,
        in_specs=(flat, flat, P(None, None, dp, tensor), P(), P(), P()),
        out_specs=(flat, flat, P(dp, None)),
        check_vma=False,
    )
```
